512 devices in a mesh: blk: 16 (over y, x_hi, core), dom: 32 (over z, x_lo).
Axes of the slice: x: 4 (x_hi: 2, x_lo: 2; x = x_hi * 2 + x_lo), y: 4, z: 16, core: 2. Of those that a mesh axis runs over, the one named last changes fastest.
Arguments:
- hidden_values: bfloat16 [65536, 256], P(('blk', 'dom')), may hold values from -6 to 6
- node_scale: float32 [65536], P(('blk', 'dom')), may hold values from 0.25 to 2
- node_weight: int32 [65536], P(('blk', 'dom')), may hold values from 8 to 24
- weight: bfloat16 [256, 256], replicated, may hold values from -0.375 to 0.375
- cotangent: bfloat16 [65536, 256], P(('blk', 'dom')), may hold values from -6 to 6
- block_rows: int32 [16, 32, 96], P('blk', 'dom'), may hold values from 0 to 31
- block_cols: int32 [16, 32, 96], P('blk', 'dom'), may hold values from 0 to 15
- block_count: int32 [16, 32], P('blk', 'dom'), may hold values from 1 to 96, as said below
- edge_counts: bfloat16 [16, 32, 96, 128, 128], P('blk', 'dom'), may hold values from 0 to 3, as said below
Outputs:
- activated: bfloat16 [65536, 256], P(('blk', 'dom'))
- grad_hidden: bfloat16 [65536, 256], P(('blk', 'dom'))
The draws below stay inside these ranges and needn't reach their ends.
Inputs may be any that keep to these rules, and one draw needn't show every extreme that they name: The first block_count[b, d] slots of a device hold its blocks and the others are unused; some device uses all 96 slots. `edge_counts`: whole numbers of edges; most entries of a block are zero.
All inputs are finite; a program needn't handle non-finite values.
Results may differ from the reference program's by a relative error of at most 0.028.
Values may be sent and summed in bfloat16 or wider, within the bound.
No kernel may reach another device: no remote copies, remote signals or barrier semaphores. Data moves between devices by JAX's collectives and lax.ppermute only.
A program may use at most 64 MiB of HBM per device.

```python
import math
import jax
import jax.numpy as jnp
from jax import lax

HID = 256
BSZ = 128
BLK_DEV = 1
SLOTS = 96
QDEN = 192
ROWBLK = 32
COLBLK = 16
NODES = 65536
N_BLK = 16
N_DOM = 32


def draw_block_count(key, part):
    key = jax.random.fold_in(key, 11)
    count_key, place_key = jax.random.split(key)
    counts = jax.random.randint(count_key, (N_BLK * N_DOM,), 1, SLOTS + 1)
    chosen = jax.random.randint(place_key, (), 0, N_BLK * N_DOM)
    flattened = jnp.where(jnp.arange(N_BLK * N_DOM) == chosen, SLOTS, counts)
    return flattened.reshape(N_BLK, N_DOM).astype(jnp.int32)


def draw_edge_counts(key, part):
    key = jax.random.fold_in(key, 23)
    levels = jax.random.randint(key, (N_BLK, N_DOM, SLOTS, BSZ, BSZ), 0, 1000)
    edges = (levels < 15).astype(jnp.int32) + (levels < 3).astype(jnp.int32) + (levels < 1).astype(jnp.int32)
    return edges.astype(jnp.float32).astype(jnp.bfloat16)


def set_ends(values, key, least, top_value):
    longest = values.shape.index(max(values.shape))
    spots = []
    for shift in (0, 1):
        where = [jax.random.randint(jax.random.fold_in(key, axis), (), 0, length) for axis, length in enumerate(values.shape)]
        where[longest] = (where[longest] + shift) % values.shape[longest]
        spots.append(tuple(where))
    return values.at[spots[0]].set(least).at[spots[1]].set(top_value)


def block_levels(key, extent, pieces, least, largest):
    factor_of, own = 1.0, jax.random.fold_in(key, 6)
    for position, blocks in pieces:
        steps = jnp.exp(jax.random.uniform(jax.random.fold_in(own, position), (blocks,), jnp.float32, least / len(pieces), largest / len(pieces)))
        factor_of = factor_of * jnp.repeat(steps, extent[position] // blocks).reshape([-1 if axis == position else 1 for axis in range(len(extent))])
    return factor_of


def noise(own_key, shape, width, reach, cuts=(), kind=jnp.bfloat16):
    factor_of = block_levels(own_key, shape, cuts, -0.22, 0.18) if cuts else 1.0
    values = jax.random.normal(own_key, shape, jnp.float32) * width * factor_of
    return jnp.minimum(jnp.maximum(values, -reach), reach).astype(kind)


def setup_inputs(seed: int = 0) -> dict:
    key_of = jax.random.split(jax.random.key(seed), 10)
    return {
        "hidden_values": noise(key_of[0], (NODES, HID), 1.0, 6.0, ((0, 512),)),
        "node_scale": jnp.clip(jnp.exp(math.log(2.0) - 2.0794415 * jax.random.uniform(key_of[1], (NODES,), jnp.float32) ** block_levels(key_of[1], (NODES,), ((0, 512),), -0.2, 0.2)), 0.25, 2.0),
        "node_weight": set_ends(jax.random.randint(key_of[2], (NODES,), 8, 25), jax.random.fold_in(key_of[2], 1), 8, 24).astype(jnp.int32),
        "weight": noise(key_of[3], (HID, HID), HID ** -0.5, 0.375),
        "cotangent": noise(key_of[4], (NODES, HID), 1.0, 6.0, ((0, 512),)),
        "block_rows": set_ends(jax.random.randint(key_of[5], (N_BLK, N_DOM, SLOTS), 0, ROWBLK), jax.random.fold_in(key_of[5], 1), 0, ROWBLK - 1).astype(jnp.int32),
        "block_cols": set_ends(jax.random.randint(key_of[6], (N_BLK, N_DOM, SLOTS), 0, COLBLK), jax.random.fold_in(key_of[6], 1), 0, COLBLK - 1).astype(jnp.int32),
        "block_count": draw_block_count(jax.random.fold_in(key_of[9], 71), 0),
        "edge_counts": draw_edge_counts(jax.random.fold_in(key_of[9], 71), 0),
    }


def reference(hidden_values, node_scale, node_weight, weight, cotangent, block_rows, block_cols, block_count, edge_counts):
    device_total = N_BLK * N_DOM
    node_norm = node_weight.astype(jnp.float32) / QDEN
    scaled = (hidden_values.astype(jnp.float32) * (node_scale * node_norm)[:, None]).astype(jnp.bfloat16)
    by_owner = scaled.reshape(N_BLK, N_DOM, BLK_DEV * BSZ, HID)
    rows_flat = block_rows.reshape(device_total, SLOTS)
    cols_flat = block_cols.reshape(device_total, SLOTS)
    count_flat = block_count.reshape(device_total)
    edges_flat = edge_counts.reshape(device_total, SLOTS, BSZ, BSZ)
    slot_ids = jnp.arange(SLOTS, dtype=jnp.int32)
    device_ids = jnp.arange(device_total, dtype=jnp.int32)

    def live_edges(device_index):
        kept_slots = (slot_ids < count_flat[device_index])[:, None, None]
        block_values = edges_flat[device_index].astype(jnp.float32)
        return jnp.where(kept_slots, block_values, jnp.zeros_like(block_values))

    def forward_step(running, device_index):
        owner_group = device_index // N_DOM
        column_dom = device_index % N_DOM
        column_set = lax.dynamic_index_in_dim(by_owner, column_dom, 1, keepdims=False)
        column_set = column_set.reshape(COLBLK, BSZ, HID)
        tile_rows = column_set[cols_flat[device_index]].astype(jnp.float32)
        contrib = jnp.einsum("kji,kjh->kih", live_edges(device_index), tile_rows)
        partial_value = jnp.zeros((ROWBLK, BSZ, HID), jnp.float32).at[rows_flat[device_index]].add(contrib)
        partial_value = lax.optimization_barrier(partial_value.astype(jnp.bfloat16)).astype(jnp.float32)
        current = lax.dynamic_index_in_dim(running, owner_group, 0, keepdims=False)
        running = lax.dynamic_update_index_in_dim(running, current + partial_value, owner_group, 0)
        return running, None

    totals, unused = lax.scan(forward_step, jnp.zeros((N_BLK, ROWBLK, BSZ, HID), jnp.float32), device_ids)
    aggregated = (totals.reshape(NODES, HID) * node_norm[:, None]).astype(jnp.bfloat16)
    preact = jnp.dot(aggregated, weight, preferred_element_type=jnp.float32)
    activated = jax.nn.silu(preact).astype(jnp.bfloat16)
    sigmoid_pre = jax.nn.sigmoid(preact)
    slope_factor = sigmoid_pre * (1.0 + preact * (1.0 - sigmoid_pre))
    dpre = (cotangent.astype(jnp.float32) * slope_factor).astype(jnp.bfloat16)
    back_rows = (jnp.dot(dpre, weight.T, preferred_element_type=jnp.float32) * node_norm[:, None]).astype(jnp.bfloat16)
    by_group = back_rows.reshape(N_BLK, ROWBLK, BSZ, HID)

    def backward_step(running, device_index):
        owner_group = device_index // N_DOM
        column_dom = device_index % N_DOM
        row_set = lax.dynamic_index_in_dim(by_group, owner_group, 0, keepdims=False)
        tile_rows = row_set[rows_flat[device_index]].astype(jnp.float32)
        contrib = jnp.einsum("kji,kih->kjh", live_edges(device_index), tile_rows)
        partial_value = jnp.zeros((COLBLK, BSZ, HID), jnp.float32).at[cols_flat[device_index]].add(contrib)
        partial_value = lax.optimization_barrier(partial_value.astype(jnp.bfloat16)).astype(jnp.float32)
        partial_value = partial_value.reshape(N_BLK, 1, BLK_DEV * BSZ, HID)
        current = lax.dynamic_slice_in_dim(running, column_dom, 1, axis=1)
        running = lax.dynamic_update_slice_in_dim(running, current + partial_value, column_dom, axis=1)
        return running, None

    grad_sums, unused = lax.scan(backward_step, jnp.zeros((N_BLK, N_DOM, BLK_DEV * BSZ, HID), jnp.float32), device_ids)
    grad_hidden = (grad_sums.reshape(NODES, HID) * node_norm[:, None]).astype(jnp.bfloat16)
    return activated, grad_hidden
```

```python
import functools

import jax
import jax.numpy as jnp
from jax import lax
from jax.experimental import pallas as pl
from jax.experimental.pallas import tpu as pltpu
from jax.sharding import Mesh, PartitionSpec as P

HID = 256
BSZ = 128
QDEN = 192
GROUP = 4
CHUNK = 16

NAMES = ("y", "xh", "core", "zh", "zl", "xl")
BLK = ("y", "xh", "core")
DOM = ("zh", "zl", "xl")


def spmm_kernel(
    transposed, count_ref, src_ref, dst_ref, edges_ref, first_ref, second_ref, out_ref, edge_buf, table, acc, sems
):
    slots = edge_buf.shape[0]
    count = count_ref[0]
    half = first_ref.shape[0]
    blocks = out_ref.shape[0]
    for c in range(slots // CHUNK):

        @pl.when(c * CHUNK < count)
        def _():
            part = pl.ds(c * CHUNK, CHUNK)
            pltpu.make_async_copy(edges_ref.at[part], edge_buf.at[part], sems.at[c]).start()

    if second_ref is not None:
        table[:half] = first_ref[...]
        table[half:] = second_ref[...]
        source = table
    else:
        source = first_ref
    acc[...] = jnp.zeros_like(acc)
    contract = (((0,), (0,)), ((), ())) if transposed else (((1,), (0,)), ((), ()))

    for c in range(slots // CHUNK):

        @pl.when(c * CHUNK < count)
        def _():
            part = pl.ds(c * CHUNK, CHUNK)
            pltpu.make_async_copy(edges_ref.at[part], edge_buf.at[part], sems.at[c]).wait()

            def step(g, carry):
                base = c * CHUNK + g * GROUP
                products = []
                for u in range(GROUP):
                    k = base + u
                    products.append(
                        lax.dot_general(
                            edge_buf[k], source[src_ref[k]], contract, preferred_element_type=jnp.float32
                        )
                    )
                for u in range(GROUP):
                    k = base + u
                    place = jnp.where(k < count, dst_ref[k], blocks)
                    acc[place] += products[u]
                return carry

            lax.fori_loop(0, CHUNK // GROUP, step, 0)

    out_ref[...] = acc[:blocks].astype(jnp.bfloat16)


def spmm(transposed, count, src, dst, edges, first, second, blocks):
    slots = edges.shape[0]
    vmem = pl.BlockSpec(memory_space=pltpu.VMEM)
    smem = pl.BlockSpec(memory_space=pltpu.SMEM)
    tables = [first] if second is None else [first, second]

    def body(count_ref, src_ref, dst_ref, edges_ref, *rest):
        first_ref = rest[0]
        second_ref = None if second is None else rest[1]
        out_ref, edge_buf, table, acc, sems = rest[len(tables) :]
        spmm_kernel(
            transposed, count_ref, src_ref, dst_ref, edges_ref, first_ref, second_ref, out_ref, edge_buf, table, acc, sems
        )

    table_rows = 1 if second is None else 2 * first.shape[0]
    return pl.pallas_call(
        body,
        out_shape=jax.ShapeDtypeStruct((blocks, BSZ, HID), jnp.bfloat16),
        in_specs=[smem, smem, smem, pl.BlockSpec(memory_space=pl.ANY)] + [vmem] * len(tables),
        out_specs=vmem,
        scratch_shapes=[
            pltpu.VMEM((slots, BSZ, BSZ), jnp.bfloat16),
            pltpu.VMEM((table_rows, BSZ, HID), jnp.bfloat16),
            pltpu.VMEM((blocks + 1, BSZ, HID), jnp.float32),
            pltpu.SemaphoreType.DMA((slots // CHUNK,)),
        ],
        compiler_params=pltpu.CompilerParams(vmem_limit_bytes=32 * 1024 * 1024),
        cost_estimate=pl.CostEstimate(
            flops=2 * slots * BSZ * BSZ * HID, bytes_accessed=2 * slots * BSZ * BSZ, transcendentals=0
        ),
    )(count, src, dst, edges, *tables)


def middle_kernel(parts_ref, norm_ref, weight_ref, cotangent_ref, activated_ref, back_ref):
    total = jnp.sum(parts_ref[...].astype(jnp.float32), axis=0)
    norm = norm_ref[...]
    aggregated = (total * norm).astype(jnp.bfloat16)
    weight = weight_ref[...]
    preact = jnp.dot(aggregated, weight, preferred_element_type=jnp.float32)
    gate = jax.nn.sigmoid(preact)
    activated_ref[...] = (preact * gate).astype(jnp.bfloat16)
    slope = gate * (1.0 + preact * (1.0 - gate))
    dpre = (cotangent_ref[...].astype(jnp.float32) * slope).astype(jnp.bfloat16)
    back = lax.dot_general(dpre, weight, (((1,), (1,)), ((), ())), preferred_element_type=jnp.float32)
    back = (back * norm).astype(jnp.bfloat16)
    for i in range(back_ref.shape[0]):
        back_ref[i] = back


def middle(parts, norm, weight, cotangent, copies):
    vmem = pl.BlockSpec(memory_space=pltpu.VMEM)
    return pl.pallas_call(
        middle_kernel,
        out_shape=(
            jax.ShapeDtypeStruct(cotangent.shape, jnp.bfloat16),
            jax.ShapeDtypeStruct((copies,) + cotangent.shape, jnp.bfloat16),
        ),
        in_specs=[vmem] * 4,
        out_specs=(vmem, vmem),
    )(parts, norm, weight, cotangent)


def exchange(value, axes):
    return lax.all_to_all(value, axes, 0, 0, tiled=True)


def other_core(value):
    return lax.ppermute(value, "core", [(0, 1), (1, 0)])


def add_up(value):
    return jnp.sum(value.astype(jnp.float32), axis=0)


def per_device(
    hidden_values, node_scale, node_weight, weight, cotangent, block_rows, block_cols, block_count, edge_counts
):
    core = lax.axis_index("core")
    node_norm = node_weight.astype(jnp.float32) / QDEN
    norm = node_norm[:, None]
    scaled = (hidden_values.astype(jnp.float32) * (node_scale * node_norm)[:, None]).astype(jnp.bfloat16)
    edges = edge_counts[0, 0]
    rows = block_rows[0, 0]
    cols = block_cols[0, 0]
    count = block_count[0]
    row_at = (rows & 3) * 8 + (rows >> 2)
    col_at = ((cols & 1) ^ core) * 8 + (cols >> 1)

    mine = exchange(jnp.broadcast_to(scaled[None], (8, BSZ, HID)), ("y", "xh"))
    theirs = other_core(mine)
    partial = spmm(True, count, col_at, row_at, edges, mine, theirs, 32)
    near = exchange(partial, ("zl", "xl"))
    near = add_up(near.reshape(4, 8, BSZ, HID)).astype(jnp.bfloat16)
    far = exchange(near, ("zh",))
    activated, back = middle(far, norm, weight, cotangent, 8)

    back = exchange(back, ("zh",))
    back = exchange(jnp.broadcast_to(back[None], (4, 8, BSZ, HID)).reshape(32, BSZ, HID), ("zl", "xl"))
    partial = spmm(False, count, row_at, col_at, edges, back, None, 16)
    received = other_core(partial[8:])
    pair = (partial[:8].astype(jnp.float32) + received.astype(jnp.float32)).astype(jnp.bfloat16)
    pair = exchange(pair, ("y", "xh"))
    grad_hidden = (add_up(pair) * norm).astype(jnp.bfloat16)
    return activated, grad_hidden


def solution(mesh):
    fine = Mesh(mesh.devices.reshape(4, 2, 2, 8, 2, 2), NAMES)
    return jax.shard_map(
        per_device,
        mesh=fine,
        in_specs=(
            P(BLK + DOM, None),
            P(BLK + DOM),
            P(BLK + DOM),
            P(),
            P(BLK + DOM, None),
            P(BLK, DOM, None),
            P(BLK, DOM, None),
            P(BLK, DOM),
            P(BLK, DOM, None, None, None),
        ),
        out_specs=(P(BLK + DOM, None), P(BLK + DOM, None)),
        check_vma=False,
    )
```

```python
import functools

import jax
import jax.numpy as jnp
from jax import lax
from jax.experimental import pallas as pl
from jax.experimental.pallas import tpu as pltpu
from jax.sharding import Mesh, PartitionSpec as P

HID = 256
BSZ = 128
QDEN = 192
GROUP = 4
CHUNK = 16

NAMES = ("y", "xh", "core", "zh", "zl", "xl")
BLK = ("y", "xh", "core")
DOM = ("zh", "zl", "xl")


def spmm_kernel(
    transposed, count_ref, src_ref, dst_ref, edges_ref, first_ref, second_ref, out_ref, edge_buf, table, acc, sems
):
    slots = edge_buf.shape[0]
    count = count_ref[0]
    half = first_ref.shape[0]
    blocks = out_ref.shape[0]
    for c in range(slots // CHUNK):

        @pl.when(c * CHUNK < count)
        def _():
            part = pl.ds(c * CHUNK, CHUNK)
            pltpu.make_async_copy(edges_ref.at[part], edge_buf.at[part], sems.at[c]).start()

    if second_ref is not None:
        table[:half] = first_ref[...]
        table[half:] = second_ref[...]
        source = table
    else:
        source = first_ref
    acc[...] = jnp.zeros_like(acc)
    contract = (((0,), (0,)), ((), ())) if transposed else (((1,), (0,)), ((), ()))

    for c in range(slots // CHUNK):

        @pl.when(c * CHUNK < count)
        def _():
            part = pl.ds(c * CHUNK, CHUNK)
            pltpu.make_async_copy(edges_ref.at[part], edge_buf.at[part], sems.at[c]).wait()

            def step(g, carry):
                base = c * CHUNK + g * GROUP
                products = []
                for u in range(GROUP):
                    k = base + u
                    products.append(
                        lax.dot_general(
                            edge_buf[k], source[src_ref[k]], contract, preferred_element_type=jnp.float32
                        )
                    )
                for u in range(GROUP):
                    k = base + u
                    place = jnp.where(k < count, dst_ref[k], blocks)
                    acc[place] += products[u]
                return carry

            lax.fori_loop(0, CHUNK // GROUP, step, 0)

    out_ref[...] = acc[:blocks].astype(jnp.bfloat16)


def spmm(transposed, count, src, dst, edges, first, second, blocks):
    slots = edges.shape[0]
    wide = first.shape[2]
    vmem = pl.BlockSpec(memory_space=pltpu.VMEM)
    smem = pl.BlockSpec(memory_space=pltpu.SMEM)
    tables = [first] if second is None else [first, second]

    def body(count_ref, src_ref, dst_ref, edges_ref, *rest):
        first_ref = rest[0]
        second_ref = None if second is None else rest[1]
        out_ref, edge_buf, table, acc, sems = rest[len(tables) :]
        spmm_kernel(
            transposed, count_ref, src_ref, dst_ref, edges_ref, first_ref, second_ref, out_ref, edge_buf, table, acc, sems
        )

    table_rows = 1 if second is None else 2 * first.shape[0]
    return pl.pallas_call(
        body,
        out_shape=jax.ShapeDtypeStruct((blocks, BSZ, wide), jnp.bfloat16),
        in_specs=[smem, smem, smem, pl.BlockSpec(memory_space=pltpu.HBM)] + [vmem] * len(tables),
        out_specs=vmem,
        scratch_shapes=[
            pltpu.VMEM((slots, BSZ, BSZ), jnp.bfloat16),
            pltpu.VMEM((table_rows, BSZ, wide), jnp.bfloat16),
            pltpu.VMEM((blocks + 1, BSZ, wide), jnp.float32),
            pltpu.SemaphoreType.DMA((slots // CHUNK,)),
        ],
        compiler_params=pltpu.CompilerParams(vmem_limit_bytes=57 * 1024 * 1024),
        cost_estimate=pl.CostEstimate(
            flops=16 * slots * BSZ * BSZ * HID, bytes_accessed=2 * slots * BSZ * BSZ, transcendentals=0
        ),
    )(count, src, dst, edges, *tables)


def middle_kernel(parts_ref, norm_ref, weight_ref, cotangent_ref, activated_ref, back_ref):
    total = jnp.sum(parts_ref[...].astype(jnp.float32), axis=0)
    norm = norm_ref[...]
    aggregated = (total * norm).astype(jnp.bfloat16)
    weight = weight_ref[...]
    preact = jnp.dot(aggregated, weight, preferred_element_type=jnp.float32)
    gate = jax.nn.sigmoid(preact)
    activated_ref[...] = (preact * gate).astype(jnp.bfloat16)
    slope = gate * (1.0 + preact * (1.0 - gate))
    dpre = (cotangent_ref[...].astype(jnp.float32) * slope).astype(jnp.bfloat16)
    back = lax.dot_general(dpre, weight, (((1,), (1,)), ((), ())), preferred_element_type=jnp.float32)
    back_ref[...] = (back * norm).astype(jnp.bfloat16)


def middle(parts, norm, weight, cotangent):
    vmem = pl.BlockSpec(memory_space=pltpu.VMEM)
    return pl.pallas_call(
        middle_kernel,
        out_shape=(
            jax.ShapeDtypeStruct(cotangent.shape, jnp.bfloat16),
            jax.ShapeDtypeStruct(cotangent.shape, jnp.bfloat16),
        ),
        in_specs=[vmem] * 4,
        out_specs=(vmem, vmem),
        compiler_params=pltpu.CompilerParams(vmem_limit_bytes=12 * 1024 * 1024),
    )(parts, norm, weight, cotangent)


def exchange(value, axes):
    return lax.all_to_all(value, axes, 0, 0, tiled=True)


def other_core(value):
    return lax.ppermute(value, "core", [(0, 1), (1, 0)])


def copies(value, number):
    return jnp.broadcast_to(value[None], (number,) + value.shape)


def add_up(value):
    return jnp.sum(value.astype(jnp.float32), axis=0)


def per_device(
    hidden_values, node_scale, node_weight, weight, cotangent, block_rows, block_cols, block_count, edge_counts
):
    core = lax.axis_index("core")
    node_norm = node_weight.astype(jnp.float32) / QDEN
    norm = node_norm[:, None]
    scaled = (hidden_values.astype(jnp.float32) * (node_scale * node_norm)[:, None]).astype(jnp.bfloat16)
    edges = edge_counts[0, 0]
    rows = block_rows[0, 0]
    cols = block_cols[0, 0]
    count = block_count[0]
    row_at = (rows & 3) * 8 + (rows >> 2)
    col_at = ((cols & 1) ^ core) * 8 + (cols >> 1)

    halves = (slice(0, HID // 2), slice(HID // 2, HID))
    mine = [exchange(copies(scaled[:, h], 8), ("y", "xh")) for h in halves]
    near = []
    for part in mine:
        partial = spmm(True, count, col_at, row_at, edges, part, other_core(part), 32)
        received = exchange(partial, ("zl", "xl"))
        near.append(add_up(received.reshape(4, 8, BSZ, HID // 2)).astype(jnp.bfloat16))
    far = exchange(jnp.concatenate(near, axis=2), ("zh",))
    activated, back = middle(far, norm, weight, cotangent)

    back = lax.all_gather(back, "zh", axis=0)
    grads = []
    for h in halves:
        table = exchange(copies(back[:, :, h], 4).reshape(32, BSZ, HID // 2), ("zl", "xl"))
        partial = spmm(False, count, row_at, col_at, edges, table, None, 16)
        received = other_core(partial[8:])
        pair = (partial[:8].astype(jnp.float32) + received.astype(jnp.float32)).astype(jnp.bfloat16)
        pair = exchange(pair, ("y", "xh"))
        grads.append((add_up(pair) * norm).astype(jnp.bfloat16))
    grad_hidden = jnp.concatenate(grads, axis=1)
    return activated, grad_hidden


def solution(mesh):
    fine = Mesh(mesh.devices.reshape(4, 2, 2, 8, 2, 2), NAMES)
    return jax.shard_map(
        per_device,
        mesh=fine,
        in_specs=(
            P(BLK + DOM, None),
            P(BLK + DOM),
            P(BLK + DOM),
            P(),
            P(BLK + DOM, None),
            P(BLK, DOM, None),
            P(BLK, DOM, None),
            P(BLK, DOM),
            P(BLK, DOM, None, None, None),
        ),
        out_specs=(P(BLK + DOM, None), P(BLK + DOM, None)),
        check_vma=False,
    )
```

```python
import functools

import jax
import jax.numpy as jnp
from jax import lax
from jax.experimental import pallas as pl
from jax.experimental.pallas import tpu as pltpu
from jax.sharding import Mesh, PartitionSpec as P

HID = 256
BSZ = 128
QDEN = 192
GROUP = 16
AHEAD = 1
CHUNK = 16

NAMES = ("y", "xh", "core", "zh", "zl", "xl")
BLK = ("y", "xh", "core")
DOM = ("zh", "zl", "xl")


def spmm_kernel(
    transposed, count_ref, src_ref, dst_ref, edges_ref, first_ref, second_ref, out_ref, edge_buf, table, acc, sems
):
    slots = edge_buf.shape[0]
    count = count_ref[0]
    half = first_ref.shape[0]
    blocks = out_ref.shape[0]
    for c in range(slots // CHUNK):

        @pl.when(c * CHUNK < count)
        def _():
            part = pl.ds(c * CHUNK, CHUNK)
            pltpu.make_async_copy(edges_ref.at[part], edge_buf.at[part], sems.at[c]).start()

    if second_ref is not None:
        table[:half] = first_ref[...]
        table[half:] = second_ref[...]
        source = table
    else:
        source = first_ref
    acc[...] = jnp.zeros_like(acc)
    contract = (((0,), (0,)), ((), ())) if transposed else (((1,), (0,)), ((), ()))

    for c in range(slots // CHUNK):

        @pl.when(c * CHUNK < count)
        def _():
            part = pl.ds(c * CHUNK, CHUNK)
            pltpu.make_async_copy(edges_ref.at[part], edge_buf.at[part], sems.at[c]).wait()

            def step(g, carry):
                base = c * CHUNK + g * GROUP
                products = []
                for u in range(GROUP + AHEAD):
                    if u < GROUP:
                        k = base + u
                        products.append(
                            lax.dot_general(
                                edge_buf[k], source[src_ref[k]], contract, preferred_element_type=jnp.float32
                            )
                        )
                    if u >= AHEAD:
                        k = base + u - AHEAD
                        place = jnp.where(k < count, dst_ref[k], blocks)
                        acc[place] += products[u - AHEAD]
                return carry

            lax.fori_loop(0, CHUNK // GROUP, step, 0)

    out_ref[...] = acc[:blocks].astype(jnp.bfloat16)


def spmm(transposed, count, src, dst, edges, first, second, blocks):
    slots = edges.shape[0]
    vmem = pl.BlockSpec(memory_space=pltpu.VMEM)
    smem = pl.BlockSpec(memory_space=pltpu.SMEM)
    tables = [first] if second is None else [first, second]

    def body(count_ref, src_ref, dst_ref, edges_ref, *rest):
        first_ref = rest[0]
        second_ref = None if second is None else rest[1]
        out_ref, edge_buf, table, acc, sems = rest[len(tables) :]
        spmm_kernel(
            transposed, count_ref, src_ref, dst_ref, edges_ref, first_ref, second_ref, out_ref, edge_buf, table, acc, sems
        )

    table_rows = 1 if second is None else 2 * first.shape[0]
    return pl.pallas_call(
        body,
        out_shape=jax.ShapeDtypeStruct((blocks, BSZ, HID), jnp.bfloat16),
        in_specs=[smem, smem, smem, pl.BlockSpec(memory_space=pl.ANY)] + [vmem] * len(tables),
        out_specs=vmem,
        scratch_shapes=[
            pltpu.VMEM((slots, BSZ, BSZ), jnp.bfloat16),
            pltpu.VMEM((table_rows, BSZ, HID), jnp.bfloat16),
            pltpu.VMEM((blocks + 1, BSZ, HID), jnp.float32),
            pltpu.SemaphoreType.DMA((slots // CHUNK,)),
        ],
        compiler_params=pltpu.CompilerParams(vmem_limit_bytes=48 * 1024 * 1024),
        cost_estimate=pl.CostEstimate(
            flops=2 * slots * BSZ * BSZ * HID, bytes_accessed=2 * slots * BSZ * BSZ, transcendentals=0
        ),
    )(count, src, dst, edges, *tables)


def middle_kernel(parts_ref, norm_ref, weight_ref, cotangent_ref, activated_ref, back_ref):
    total = jnp.sum(parts_ref[...].astype(jnp.float32), axis=0)
    norm = norm_ref[...]
    aggregated = (total * norm).astype(jnp.bfloat16)
    weight = weight_ref[...]
    preact = jnp.dot(aggregated, weight, preferred_element_type=jnp.float32)
    gate = jax.nn.sigmoid(preact)
    activated_ref[...] = (preact * gate).astype(jnp.bfloat16)
    slope = gate * (1.0 + preact * (1.0 - gate))
    dpre = (cotangent_ref[...].astype(jnp.float32) * slope).astype(jnp.bfloat16)
    back = lax.dot_general(dpre, weight, (((1,), (1,)), ((), ())), preferred_element_type=jnp.float32)
    back = (back * norm).astype(jnp.bfloat16).astype(jnp.float32)
    largest = jnp.maximum(jnp.max(jnp.abs(back), axis=(0, 1), keepdims=True), 1e-30)
    power = 14.0 - jnp.floor(jnp.log2(largest))
    back_ref[:BSZ] = back * jnp.exp2(power)
    back_ref[BSZ:] = jnp.broadcast_to(power, (8, HID))


def middle(parts, norm, weight, cotangent):
    vmem = pl.BlockSpec(memory_space=pltpu.VMEM)
    return pl.pallas_call(
        middle_kernel,
        out_shape=(
            jax.ShapeDtypeStruct(cotangent.shape, jnp.bfloat16),
            jax.ShapeDtypeStruct((BSZ + 8, HID), jnp.float32),
        ),
        in_specs=[vmem] * 4,
        out_specs=(vmem, vmem),
        compiler_params=pltpu.CompilerParams(vmem_limit_bytes=12 * 1024 * 1024),
    )(parts, norm, weight, cotangent)


def exchange(value, axes):
    return lax.all_to_all(value, axes, 0, 0, tiled=True)


def other_core(value):
    return lax.ppermute(value, "core", [(0, 1), (1, 0)])


def gather_scaled(value):
    sent = value.astype(jnp.float16)
    pair = jnp.concatenate([sent, lax.ppermute(sent, "xl", [(0, 1), (1, 0)])], axis=0)
    pairs = lax.all_gather(pair, ("zh", "zl"), axis=0, tiled=True).reshape(32, BSZ + 8, HID)
    back = jnp.exp2(-pairs[:, BSZ : BSZ + 1, :1].astype(jnp.float32))
    return (pairs[:, :BSZ].astype(jnp.float32) * back).astype(jnp.bfloat16)


def add_up(value):
    return jnp.sum(value.astype(jnp.float32), axis=0)


def per_device(
    hidden_values, node_scale, node_weight, weight, cotangent, block_rows, block_cols, block_count, edge_counts
):
    core = lax.axis_index("core")
    node_norm = node_weight.astype(jnp.float32) / QDEN
    norm = node_norm[:, None]
    scaled = (hidden_values.astype(jnp.float32) * (node_scale * node_norm)[:, None]).astype(jnp.bfloat16)
    edges = edge_counts[0, 0]
    rows = block_rows[0, 0]
    cols = block_cols[0, 0]
    count = block_count[0]
    row_at = (rows & 3) * 8 + (rows >> 2)
    row_to = (rows & ~1) + ((rows & 1) ^ lax.axis_index("xl"))
    col_at = ((cols & 1) ^ core) * 8 + (cols >> 1)

    mine = exchange(jnp.broadcast_to(scaled[None], (8, BSZ, HID)), ("y", "xh"))
    theirs = other_core(mine)
    partial = spmm(True, count, col_at, row_at, edges, mine, theirs, 32)
    near = exchange(partial, ("zl", "xl"))
    near = add_up(near.reshape(4, 8, BSZ, HID)).astype(jnp.bfloat16)
    far = exchange(near, ("zh",))
    activated, back = middle(far, norm, weight, cotangent)

    table = gather_scaled(back)
    partial = spmm(False, count, row_to, col_at, edges, table, None, 16)
    received = other_core(partial[8:])
    pair = (partial[:8].astype(jnp.float32) + received.astype(jnp.float32)).astype(jnp.bfloat16)
    pair = exchange(pair, ("y", "xh"))
    grad_hidden = (add_up(pair) * norm).astype(jnp.bfloat16)
    return activated, grad_hidden


def solution(mesh):
    fine = Mesh(mesh.devices.reshape(4, 2, 2, 8, 2, 2), NAMES)
    return jax.shard_map(
        per_device,
        mesh=fine,
        in_specs=(
            P(BLK + DOM, None),
            P(BLK + DOM),
            P(BLK + DOM),
            P(),
            P(BLK + DOM, None),
            P(BLK, DOM, None),
            P(BLK, DOM, None),
            P(BLK, DOM),
            P(BLK, DOM, None, None, None),
        ),
        out_specs=(P(BLK + DOM, None), P(BLK + DOM, None)),
        check_vma=False,
    )
```

```python
import functools

import jax
import jax.numpy as jnp
from jax import lax
from jax.experimental import pallas as pl
from jax.experimental.pallas import tpu as pltpu
from jax.sharding import Mesh, PartitionSpec as P

HID = 256
BSZ = 128
QDEN = 192
GROUP = 32
AHEAD = 1
CHUNK = 32

NAMES = ("y", "xh", "core", "zh", "zl", "xl")
BLK = ("y", "xh", "core")
DOM = ("zh", "zl", "xl")


def spmm_kernel(
    transposed, count_ref, src_ref, dst_ref, edges_ref, first_ref, second_ref, out_ref, edge_buf, table, acc, sems
):
    slots = edge_buf.shape[0]
    count = count_ref[0]
    half = first_ref.shape[0]
    blocks = out_ref.shape[0]
    for c in range(slots // CHUNK):

        @pl.when(c * CHUNK < count)
        def _():
            part = pl.ds(c * CHUNK, CHUNK)
            pltpu.make_async_copy(edges_ref.at[part], edge_buf.at[part], sems.at[c]).start()

    if second_ref is not None:
        table[:half] = first_ref[...]
        table[half:] = second_ref[...]
        source = table
    else:
        source = first_ref
    acc[...] = jnp.zeros_like(acc)
    contract = (((0,), (0,)), ((), ())) if transposed else (((1,), (0,)), ((), ()))

    for c in range(slots // CHUNK):

        @pl.when(c * CHUNK < count)
        def _():
            part = pl.ds(c * CHUNK, CHUNK)
            pltpu.make_async_copy(edges_ref.at[part], edge_buf.at[part], sems.at[c]).wait()

            def step(g, carry):
                base = c * CHUNK + g * GROUP
                products = []
                for u in range(GROUP + AHEAD):
                    if u < GROUP:
                        k = base + u
                        products.append(
                            lax.dot_general(
                                edge_buf[k], source[src_ref[k]], contract, preferred_element_type=jnp.float32
                            )
                        )
                    if u >= AHEAD:
                        k = base + u - AHEAD
                        place = jnp.where(k < count, dst_ref[k], blocks)
                        acc[place] += products[u - AHEAD]
                return carry

            lax.fori_loop(0, CHUNK // GROUP, step, 0)

    out_ref[...] = acc[:blocks].astype(jnp.bfloat16)


def spmm(transposed, count, src, dst, edges, first, second, blocks):
    slots = edges.shape[0]
    vmem = pl.BlockSpec(memory_space=pltpu.VMEM)
    smem = pl.BlockSpec(memory_space=pltpu.SMEM)
    tables = [first] if second is None else [first, second]

    def body(count_ref, src_ref, dst_ref, edges_ref, *rest):
        first_ref = rest[0]
        second_ref = None if second is None else rest[1]
        out_ref, edge_buf, table, acc, sems = rest[len(tables) :]
        spmm_kernel(
            transposed, count_ref, src_ref, dst_ref, edges_ref, first_ref, second_ref, out_ref, edge_buf, table, acc, sems
        )

    table_rows = 1 if second is None else 2 * first.shape[0]
    return pl.pallas_call(
        body,
        out_shape=jax.ShapeDtypeStruct((blocks, BSZ, HID), jnp.bfloat16),
        in_specs=[smem, smem, smem, pl.BlockSpec(memory_space=pl.ANY)] + [vmem] * len(tables),
        out_specs=vmem,
        scratch_shapes=[
            pltpu.VMEM((slots, BSZ, BSZ), jnp.bfloat16),
            pltpu.VMEM((table_rows, BSZ, HID), jnp.bfloat16),
            pltpu.VMEM((blocks + 1, BSZ, HID), jnp.float32),
            pltpu.SemaphoreType.DMA((slots // CHUNK,)),
        ],
        compiler_params=pltpu.CompilerParams(vmem_limit_bytes=48 * 1024 * 1024),
        cost_estimate=pl.CostEstimate(
            flops=2 * slots * BSZ * BSZ * HID, bytes_accessed=2 * slots * BSZ * BSZ, transcendentals=0
        ),
    )(count, src, dst, edges, *tables)


def per_row(row):
    square = jnp.broadcast_to(row, (BSZ, BSZ)).T
    return jnp.concatenate([square] * (HID // BSZ), axis=1)


def norm_of(counts_ref):
    return counts_ref[...].astype(jnp.float32) / QDEN


def end_kernel(parts_ref, counts_ref, out_ref):
    total = jnp.sum(parts_ref[...].astype(jnp.float32), axis=0)
    out_ref[...] = (total * per_row(norm_of(counts_ref))).astype(jnp.bfloat16)


def small_call(kernel, out_shape, *operands):
    vmem = pl.BlockSpec(memory_space=pltpu.VMEM)
    return pl.pallas_call(
        kernel,
        out_shape=out_shape,
        in_specs=[vmem] * len(operands),
        out_specs=jax.tree.map(lambda _: vmem, out_shape),
        compiler_params=pltpu.CompilerParams(vmem_limit_bytes=12 * 1024 * 1024),
    )(*operands)


def middle_kernel(parts_ref, counts_ref, weight_ref, cotangent_ref, activated_ref, back_ref):
    total = jnp.sum(parts_ref[...].astype(jnp.float32), axis=0)
    norm = per_row(norm_of(counts_ref))
    aggregated = (total * norm).astype(jnp.bfloat16)
    weight = weight_ref[...]
    preact = jnp.dot(aggregated, weight, preferred_element_type=jnp.float32)
    gate = jax.nn.sigmoid(preact)
    activated_ref[...] = (preact * gate).astype(jnp.bfloat16)
    slope = gate * (1.0 + preact * (1.0 - gate))
    dpre = (cotangent_ref[...].astype(jnp.float32) * slope).astype(jnp.bfloat16)
    back = lax.dot_general(dpre, weight, (((1,), (1,)), ((), ())), preferred_element_type=jnp.float32)
    back = (back * norm).astype(jnp.bfloat16).astype(jnp.float32)
    largest = jnp.maximum(jnp.max(jnp.abs(back), axis=(0, 1), keepdims=True), 1e-30)
    power = 14.0 - jnp.floor(jnp.log2(largest))
    back_ref[:BSZ] = back * jnp.exp2(power)
    back_ref[BSZ:] = jnp.broadcast_to(power, (8, HID))


def exchange(value, axes):
    return lax.all_to_all(value, axes, 0, 0, tiled=True)


def other_core(value):
    return lax.ppermute(value, "core", [(0, 1), (1, 0)])


def gather_scaled(value):
    sent = value.astype(jnp.float16)
    pair = jnp.concatenate([sent, lax.ppermute(sent, "xl", [(0, 1), (1, 0)])], axis=0)
    pairs = lax.all_gather(pair, ("zh", "zl"), axis=0, tiled=True).reshape(32, BSZ + 8, HID)
    back = jnp.exp2(-pairs[:, BSZ : BSZ + 1, :1].astype(jnp.float32))
    return (pairs[:, :BSZ].astype(jnp.float32) * back).astype(jnp.bfloat16)


def add_up(value):
    return jnp.sum(value.astype(jnp.float32), axis=0)


def per_device(
    hidden_values, node_scale, node_weight, weight, cotangent, block_rows, block_cols, block_count, edge_counts
):
    core = lax.axis_index("core")
    counts = node_weight[None, :]
    edges = edge_counts[0, 0]
    rows = block_rows[0, 0]
    cols = block_cols[0, 0]
    count = block_count[0]
    row_at = (rows & 3) * 8 + (rows >> 2)
    row_to = (rows & ~1) + ((rows & 1) ^ lax.axis_index("xl"))
    col_at = ((cols & 1) ^ core) * 8 + (cols >> 1)

    factor = node_scale * (node_weight.astype(jnp.float32) / QDEN)
    scaled = (hidden_values.astype(jnp.float32) * factor[:, None]).astype(jnp.bfloat16)
    mine = exchange(jnp.broadcast_to(scaled[None], (8, BSZ, HID)), ("y", "xh"))
    theirs = other_core(mine)
    partial = spmm(True, count, col_at, row_at, edges, mine, theirs, 32)
    near = exchange(partial, ("zl", "xl"))
    near = add_up(near.reshape(4, 8, BSZ, HID)).astype(jnp.bfloat16)
    far = exchange(near, ("zh",))
    own = jax.ShapeDtypeStruct((BSZ, HID), jnp.bfloat16)
    sent = jax.ShapeDtypeStruct((BSZ + 8, HID), jnp.float32)
    activated, back = small_call(middle_kernel, (own, sent), far, counts, weight, cotangent)

    table = gather_scaled(back)
    partial = spmm(False, count, row_to, col_at, edges, table, None, 16)
    received = other_core(partial[8:])
    pair = (partial[:8].astype(jnp.float32) + received.astype(jnp.float32)).astype(jnp.bfloat16)
    pair = exchange(pair, ("y", "xh"))
    grad_hidden = small_call(end_kernel, own, pair, counts)
    return activated, grad_hidden


def solution(mesh):
    fine = Mesh(mesh.devices.reshape(4, 2, 2, 8, 2, 2), NAMES)
    return jax.shard_map(
        per_device,
        mesh=fine,
        in_specs=(
            P(BLK + DOM, None),
            P(BLK + DOM),
            P(BLK + DOM),
            P(),
            P(BLK + DOM, None),
            P(BLK, DOM, None),
            P(BLK, DOM, None),
            P(BLK, DOM),
            P(BLK, DOM, None, None, None),
        ),
        out_specs=(P(BLK + DOM, None), P(BLK + DOM, None)),
        check_vma=False,
    )
```

```python
import functools

import jax
import jax.numpy as jnp
from jax import lax
from jax.experimental import pallas as pl
from jax.experimental.pallas import tpu as pltpu
from jax.sharding import Mesh, PartitionSpec as P

HID = 256
BSZ = 128
QDEN = 192
GROUP = 32
AHEAD = 1
CHUNK = 32
SPREAD = 2 * BSZ + 16

NAMES = ("y", "xh", "core", "zh", "zl", "xl")
BLK = ("y", "xh", "core")
DOM = ("zh", "zl", "xl")


def spmm_kernel(
    transposed, count_ref, src_ref, dst_ref, edges_ref, first_ref, second_ref, out_ref, edge_buf, table, acc, sems
):
    slots = edge_buf.shape[0]
    count = count_ref[0]
    half = first_ref.shape[0]
    blocks = acc.shape[0] - 1
    for c in range(slots // CHUNK):

        @pl.when(c * CHUNK < count)
        def _():
            part = pl.ds(c * CHUNK, CHUNK)
            pltpu.make_async_copy(edges_ref.at[part], edge_buf.at[part], sems.at[c]).start()

    if second_ref is not None:
        table[:half] = first_ref[...]
        table[half:] = second_ref[...]
        source = table
    else:
        source = first_ref
    acc[...] = jnp.zeros_like(acc)
    contract = (((0,), (0,)), ((), ())) if transposed else (((1,), (0,)), ((), ()))

    for c in range(slots // CHUNK):

        @pl.when(c * CHUNK < count)
        def _():
            part = pl.ds(c * CHUNK, CHUNK)
            pltpu.make_async_copy(edges_ref.at[part], edge_buf.at[part], sems.at[c]).wait()

            def step(g, carry):
                base = c * CHUNK + g * GROUP
                products = []
                for u in range(GROUP + AHEAD):
                    if u < GROUP:
                        k = base + u
                        products.append(
                            lax.dot_general(
                                edge_buf[k], source[src_ref[k]], contract, preferred_element_type=jnp.float32
                            )
                        )
                    if u >= AHEAD:
                        k = base + u - AHEAD
                        place = jnp.where(k < count, dst_ref[k], blocks)
                        acc[place] += products[u - AHEAD]
                return carry

            lax.fori_loop(0, CHUNK // GROUP, step, 0)

    if len(out_ref.shape) == 3:
        out_ref[...] = acc[:blocks].astype(jnp.bfloat16)
    else:
        for z in range(blocks // 2):
            for h in range(2):
                out_ref[pl.ds(SPREAD * z + BSZ * h, BSZ)] = acc[2 * z + h].astype(jnp.bfloat16)
            if z < blocks // 2 - 1:
                out_ref[pl.ds(SPREAD * z + 2 * BSZ, 16)] = jnp.zeros((16, HID), jnp.bfloat16)


def spmm(transposed, count, src, dst, edges, first, second, blocks, out_shape):
    slots = edges.shape[0]
    vmem = pl.BlockSpec(memory_space=pltpu.VMEM)
    smem = pl.BlockSpec(memory_space=pltpu.SMEM)
    tables = [first] if second is None else [first, second]

    def body(count_ref, src_ref, dst_ref, edges_ref, *rest):
        first_ref = rest[0]
        second_ref = None if second is None else rest[1]
        out_ref, edge_buf, table, acc, sems = rest[len(tables) :]
        spmm_kernel(
            transposed, count_ref, src_ref, dst_ref, edges_ref, first_ref, second_ref, out_ref, edge_buf, table, acc, sems
        )

    table_rows = 1 if second is None else 2 * first.shape[0]
    return pl.pallas_call(
        body,
        out_shape=jax.ShapeDtypeStruct(out_shape, jnp.bfloat16),
        in_specs=[smem, smem, smem, pl.BlockSpec(memory_space=pl.ANY)] + [vmem] * len(tables),
        out_specs=vmem,
        scratch_shapes=[
            pltpu.VMEM((slots, BSZ, BSZ), jnp.bfloat16),
            pltpu.VMEM((table_rows, BSZ, HID), jnp.bfloat16),
            pltpu.VMEM((blocks + 1, BSZ, HID), jnp.float32),
            pltpu.SemaphoreType.DMA((slots // CHUNK,)),
        ],
        compiler_params=pltpu.CompilerParams(vmem_limit_bytes=48 * 1024 * 1024),
        cost_estimate=pl.CostEstimate(
            flops=2 * slots * BSZ * BSZ * HID, bytes_accessed=2 * slots * BSZ * BSZ, transcendentals=0
        ),
    )(count, src, dst, edges, *tables)


def per_row(row):
    square = jnp.broadcast_to(row, (BSZ, BSZ)).T
    return jnp.concatenate([square] * (HID // BSZ), axis=1)


def norm_of(counts_ref):
    return counts_ref[...].astype(jnp.float32) / QDEN


def end_kernel(parts_ref, counts_ref, out_ref):
    total = jnp.sum(parts_ref[...].astype(jnp.float32), axis=0)
    out_ref[...] = (total * per_row(norm_of(counts_ref))).astype(jnp.bfloat16)


def small_call(kernel, out_shape, *operands):
    vmem = pl.BlockSpec(memory_space=pltpu.VMEM)
    return pl.pallas_call(
        kernel,
        out_shape=out_shape,
        in_specs=[vmem] * len(operands),
        out_specs=jax.tree.map(lambda _: vmem, out_shape),
        compiler_params=pltpu.CompilerParams(vmem_limit_bytes=12 * 1024 * 1024),
    )(*operands)


def middle_kernel(mine_ref, theirs_ref, counts_ref, weight_ref, cotangent_ref, activated_ref, back_ref):
    total = mine_ref[...].astype(jnp.float32) + theirs_ref[...].astype(jnp.float32)
    norm = per_row(norm_of(counts_ref))
    aggregated = (total * norm).astype(jnp.bfloat16)
    weight = weight_ref[...]
    preact = jnp.dot(aggregated, weight, preferred_element_type=jnp.float32)
    gate = jax.nn.sigmoid(preact)
    activated_ref[...] = (preact * gate).astype(jnp.bfloat16)
    slope = gate * (1.0 + preact * (1.0 - gate))
    dpre = (cotangent_ref[...].astype(jnp.float32) * slope).astype(jnp.bfloat16)
    back = lax.dot_general(dpre, weight, (((1,), (1,)), ((), ())), preferred_element_type=jnp.float32)
    back = (back * norm).astype(jnp.bfloat16).astype(jnp.float32)
    largest = jnp.maximum(jnp.max(jnp.abs(back), axis=(0, 1), keepdims=True), 1e-30)
    power = 14.0 - jnp.floor(jnp.log2(largest))
    back_ref[:BSZ] = back * jnp.exp2(power)
    back_ref[BSZ:] = jnp.broadcast_to(power, (8, HID))


def exchange(value, axes):
    return lax.all_to_all(value, axes, 0, 0, tiled=True)


def other_core(value):
    return lax.ppermute(value, "core", [(0, 1), (1, 0)])


def gather_scaled(value):
    sent = value.astype(jnp.float16)
    pair = jnp.concatenate([sent, other_x(sent)], axis=0)
    pairs = lax.all_gather(pair, ("zh", "zl"), axis=0, tiled=True).reshape(32, BSZ + 8, HID)
    back = jnp.exp2(-pairs[:, BSZ : BSZ + 1, :1].astype(jnp.float32))
    return (pairs[:, :BSZ].astype(jnp.float32) * back).astype(jnp.bfloat16)


def other_x(value):
    return lax.ppermute(value, "xl", [(0, 1), (1, 0)])


def summed_over_z(partial):
    shard = lax.psum_scatter(partial, ("zh", "zl"), scatter_dimension=0, tiled=True)
    shard = lax.optimization_barrier(shard)
    return lax.dynamic_slice(shard, (lax.axis_index(("zh", "zl")), 0), (2 * BSZ, HID))


def per_device(
    hidden_values, node_scale, node_weight, weight, cotangent, block_rows, block_cols, block_count, edge_counts
):
    core = lax.axis_index("core")
    counts = node_weight[None, :]
    edges = edge_counts[0, 0]
    rows = block_rows[0, 0]
    cols = block_cols[0, 0]
    count = block_count[0]
    row_at = (rows & ~1) + ((rows & 1) ^ lax.axis_index("xl"))
    col_at = ((cols & 1) ^ core) * 8 + (cols >> 1)

    factor = node_scale * (node_weight.astype(jnp.float32) / QDEN)
    scaled = (hidden_values.astype(jnp.float32) * factor[:, None]).astype(jnp.bfloat16)
    mine = exchange(jnp.broadcast_to(scaled[None], (8, BSZ, HID)), ("y", "xh"))
    theirs = other_core(mine)
    partial = spmm(True, count, col_at, row_at, edges, mine, theirs, 32, (16 * (SPREAD - 1), HID))
    sums = summed_over_z(partial)
    received = other_x(sums[BSZ:])
    own = jax.ShapeDtypeStruct((BSZ, HID), jnp.bfloat16)
    sent = jax.ShapeDtypeStruct((BSZ + 8, HID), jnp.float32)
    activated, back = small_call(middle_kernel, (own, sent), sums[:BSZ], received, counts, weight, cotangent)

    table = gather_scaled(back)
    partial = spmm(False, count, row_at, col_at, edges, table, None, 16, (16, BSZ, HID))
    received = other_core(partial[8:])
    pair = (partial[:8].astype(jnp.float32) + received.astype(jnp.float32)).astype(jnp.bfloat16)
    pair = exchange(pair, ("y", "xh"))
    grad_hidden = small_call(end_kernel, own, pair, counts)
    return activated, grad_hidden


def solution(mesh):
    fine = Mesh(mesh.devices.reshape(4, 2, 2, 8, 2, 2), NAMES)
    return jax.shard_map(
        per_device,
        mesh=fine,
        in_specs=(
            P(BLK + DOM, None),
            P(BLK + DOM),
            P(BLK + DOM),
            P(),
            P(BLK + DOM, None),
            P(BLK, DOM, None),
            P(BLK, DOM, None),
            P(BLK, DOM),
            P(BLK, DOM, None, None, None),
        ),
        out_specs=(P(BLK + DOM, None), P(BLK + DOM, None)),
        check_vma=False,
    )
```

```python
import functools

import jax
import jax.numpy as jnp
from jax import lax
from jax.experimental import pallas as pl
from jax.experimental.pallas import tpu as pltpu
from jax.sharding import Mesh, PartitionSpec as P

HID = 256
BSZ = 128
QDEN = 192
GROUP = 32
AHEAD = 1
CHUNK = 32
SPREAD = 2 * BSZ + 16

NAMES = ("y", "xh", "core", "zh", "zl", "xl")
BLK = ("y", "xh", "core")
DOM = ("zh", "zl", "xl")


def spmm_kernel(
    transposed, count_ref, src_ref, dst_ref, edges_ref, first_ref, second_ref, out_ref, edge_buf, table, acc, sems
):
    slots = edge_buf.shape[0]
    count = count_ref[0]
    half = first_ref.shape[0]
    blocks = acc.shape[0] - 1
    for c in range(slots // CHUNK):

        @pl.when(c * CHUNK < count)
        def _():
            part = pl.ds(c * CHUNK, CHUNK)
            pltpu.make_async_copy(edges_ref.at[part], edge_buf.at[part], sems.at[c]).start()

    if second_ref is not None:
        table[:half] = first_ref[...]
        table[half:] = second_ref[...]
        source = table
    else:
        source = first_ref
    acc[...] = jnp.zeros_like(acc)
    contract = (((0,), (0,)), ((), ())) if transposed else (((1,), (0,)), ((), ()))

    for c in range(slots // CHUNK):

        @pl.when(c * CHUNK < count)
        def _():
            part = pl.ds(c * CHUNK, CHUNK)
            pltpu.make_async_copy(edges_ref.at[part], edge_buf.at[part], sems.at[c]).wait()

            def step(g, carry):
                base = c * CHUNK + g * GROUP
                products = []
                for u in range(GROUP + AHEAD):
                    if u < GROUP:
                        k = base + u
                        products.append(
                            lax.dot_general(
                                edge_buf[k], source[src_ref[k]], contract, preferred_element_type=jnp.float32
                            )
                        )
                    if u >= AHEAD:
                        k = base + u - AHEAD
                        place = jnp.where(k < count, dst_ref[k], blocks)
                        acc[place] += products[u - AHEAD]
                return carry

            lax.fori_loop(0, CHUNK // GROUP, step, 0)

    if len(out_ref.shape) == 3:
        out_ref[...] = acc[:blocks].astype(jnp.bfloat16)
    else:
        for z in range(blocks // 2):
            for h in range(2):
                out_ref[pl.ds(SPREAD * z + BSZ * h, BSZ)] = acc[2 * z + h].astype(jnp.bfloat16)
            if z < blocks // 2 - 1:
                out_ref[pl.ds(SPREAD * z + 2 * BSZ, 16)] = jnp.zeros((16, HID), jnp.bfloat16)


def spmm(transposed, count, src, dst, edges, first, second, blocks, out_shape):
    slots = edges.shape[0]
    vmem = pl.BlockSpec(memory_space=pltpu.VMEM)
    smem = pl.BlockSpec(memory_space=pltpu.SMEM)
    tables = [first] if second is None else [first, second]

    def body(count_ref, src_ref, dst_ref, edges_ref, *rest):
        first_ref = rest[0]
        second_ref = None if second is None else rest[1]
        out_ref, edge_buf, table, acc, sems = rest[len(tables) :]
        spmm_kernel(
            transposed, count_ref, src_ref, dst_ref, edges_ref, first_ref, second_ref, out_ref, edge_buf, table, acc, sems
        )

    table_rows = 1 if second is None else 2 * first.shape[0]
    return pl.pallas_call(
        body,
        out_shape=jax.ShapeDtypeStruct(out_shape, jnp.bfloat16),
        in_specs=[smem, smem, smem, pl.BlockSpec(memory_space=pl.ANY)] + [vmem] * len(tables),
        out_specs=vmem,
        scratch_shapes=[
            pltpu.VMEM((slots, BSZ, BSZ), jnp.bfloat16),
            pltpu.VMEM((table_rows, BSZ, HID), jnp.bfloat16),
            pltpu.VMEM((blocks + 1, BSZ, HID), jnp.float32),
            pltpu.SemaphoreType.DMA((slots // CHUNK,)),
        ],
        compiler_params=pltpu.CompilerParams(vmem_limit_bytes=48 * 1024 * 1024),
        cost_estimate=pl.CostEstimate(
            flops=2 * slots * BSZ * BSZ * HID, bytes_accessed=2 * slots * BSZ * BSZ, transcendentals=0
        ),
    )(count, src, dst, edges, *tables)


def per_row(row):
    square = jnp.broadcast_to(row, (BSZ, BSZ)).T
    return jnp.concatenate([square] * (HID // BSZ), axis=1)


def norm_of(counts_ref):
    return counts_ref[...].astype(jnp.float32) / QDEN


def end_kernel(parts_ref, counts_ref, out_ref):
    total = jnp.sum(parts_ref[...].astype(jnp.float32), axis=0)
    out_ref[...] = (total * per_row(norm_of(counts_ref))).astype(jnp.bfloat16)


def small_call(kernel, out_shape, *operands):
    vmem = pl.BlockSpec(memory_space=pltpu.VMEM)
    return pl.pallas_call(
        kernel,
        out_shape=out_shape,
        in_specs=[vmem] * len(operands),
        out_specs=jax.tree.map(lambda _: vmem, out_shape),
        compiler_params=pltpu.CompilerParams(vmem_limit_bytes=12 * 1024 * 1024),
    )(*operands)


def middle_kernel(
    sums_ref, received_ref, counts_ref, weight_ref, cotangent_ref, activated_ref, back_ref
):
    weight = weight_ref[...]
    largest = jnp.full((1, 1), 1e-30, jnp.float32)
    backs = []
    for h in range(2):
        mine = sums_ref[pl.ds(BSZ * h, BSZ)].astype(jnp.float32)
        total = mine + received_ref[pl.ds(BSZ * (1 - h), BSZ)].astype(jnp.float32)
        if h == 0:
            norm = per_row(norm_of(counts_ref))
            cotangent = cotangent_ref[...].astype(jnp.float32)
        else:
            norm = per_row(received_ref[pl.ds(3 * BSZ, 16)].astype(jnp.float32)[:1, :BSZ] / QDEN)
            cotangent = received_ref[pl.ds(2 * BSZ, BSZ)].astype(jnp.float32)
        aggregated = (total * norm).astype(jnp.bfloat16)
        preact = jnp.dot(aggregated, weight, preferred_element_type=jnp.float32)
        gate = jax.nn.sigmoid(preact)
        if h == 0:
            activated_ref[...] = (preact * gate).astype(jnp.bfloat16)
        slope = gate * (1.0 + preact * (1.0 - gate))
        dpre = (cotangent * slope).astype(jnp.bfloat16)
        back = lax.dot_general(dpre, weight, (((1,), (1,)), ((), ())), preferred_element_type=jnp.float32)
        back = (back * norm).astype(jnp.bfloat16).astype(jnp.float32)
        largest = jnp.maximum(largest, jnp.max(jnp.abs(back), axis=(0, 1), keepdims=True))
        backs.append(back)
    power = 14.0 - jnp.floor(jnp.log2(largest))
    for h in range(2):
        back_ref[pl.ds(BSZ * h, BSZ)] = backs[h] * jnp.exp2(power)
    back_ref[pl.ds(2 * BSZ, 8)] = jnp.broadcast_to(power, (8, HID))


def exchange(value, axes):
    return lax.all_to_all(value, axes, 0, 0, tiled=True)


def other_core(value):
    return lax.ppermute(value, "core", [(0, 1), (1, 0)])


def gather_scaled(value):
    sent = value.astype(jnp.float16)
    pairs = lax.all_gather(sent, ("zh", "zl"), axis=0, tiled=True).reshape(16, 2 * BSZ + 8, HID)
    back = jnp.exp2(-pairs[:, 2 * BSZ : 2 * BSZ + 1, :1].astype(jnp.float32))
    table = (pairs[:, : 2 * BSZ].astype(jnp.float32) * back).astype(jnp.bfloat16)
    return table.reshape(32, BSZ, HID)


def other_x(value):
    return lax.ppermute(value, "xl", [(0, 1), (1, 0)])


def summed_over_z(partial):
    shard = lax.psum_scatter(partial, ("zh", "zl"), scatter_dimension=0, tiled=True)
    shard = lax.optimization_barrier(shard)
    return lax.dynamic_slice(shard, (lax.axis_index(("zh", "zl")), 0), (2 * BSZ, HID))


def per_device(
    hidden_values, node_scale, node_weight, weight, cotangent, block_rows, block_cols, block_count, edge_counts
):
    core = lax.axis_index("core")
    counts = node_weight[None, :]
    edges = edge_counts[0, 0]
    rows = block_rows[0, 0]
    cols = block_cols[0, 0]
    count = block_count[0]
    row_at = (rows & ~1) + ((rows & 1) ^ lax.axis_index("xl"))
    col_at = ((cols & 1) ^ core) * 8 + (cols >> 1)

    factor = node_scale * (node_weight.astype(jnp.float32) / QDEN)
    scaled = (hidden_values.astype(jnp.float32) * factor[:, None]).astype(jnp.bfloat16)
    mine = exchange(jnp.broadcast_to(scaled[None], (8, BSZ, HID)), ("y", "xh"))
    theirs = other_core(mine)
    partial = spmm(True, count, col_at, row_at, edges, mine, theirs, 32, (16 * (SPREAD - 1), HID))
    sums = summed_over_z(partial)
    small = jnp.broadcast_to(jnp.tile(node_weight.astype(jnp.bfloat16), HID // BSZ), (16, HID))
    received = other_x(jnp.concatenate([sums, cotangent, small], axis=0))
    own = jax.ShapeDtypeStruct((BSZ, HID), jnp.bfloat16)
    sent = jax.ShapeDtypeStruct((2 * BSZ + 8, HID), jnp.float32)
    activated, back = small_call(middle_kernel, (own, sent), sums, received, counts, weight, cotangent)

    table = gather_scaled(back)
    partial = spmm(False, count, row_at, col_at, edges, table, None, 16, (16, BSZ, HID))
    received = other_core(partial[8:])
    pair = (partial[:8].astype(jnp.float32) + received.astype(jnp.float32)).astype(jnp.bfloat16)
    pair = exchange(pair, ("y", "xh"))
    grad_hidden = small_call(end_kernel, own, pair, counts)
    return activated, grad_hidden


def solution(mesh):
    fine = Mesh(mesh.devices.reshape(4, 2, 2, 8, 2, 2), NAMES)
    return jax.shard_map(
        per_device,
        mesh=fine,
        in_specs=(
            P(BLK + DOM, None),
            P(BLK + DOM),
            P(BLK + DOM),
            P(),
            P(BLK + DOM, None),
            P(BLK, DOM, None),
            P(BLK, DOM, None),
            P(BLK, DOM),
            P(BLK, DOM, None, None, None),
        ),
        out_specs=(P(BLK + DOM, None), P(BLK + DOM, None)),
        check_vma=False,
    )
```

```python
import functools

import jax
import jax.numpy as jnp
from jax import lax
from jax.experimental import pallas as pl
from jax.experimental.pallas import tpu as pltpu
from jax.sharding import Mesh, PartitionSpec as P

HID = 256
BSZ = 128
QDEN = 192
GROUP = 48
AHEAD = 1
CHUNK = 48
SPREAD = 2 * BSZ + 16

NAMES = ("y", "xh", "core", "zh", "zl", "xl")
BLK = ("y", "xh", "core")
DOM = ("zh", "zl", "xl")


def spmm_kernel(
    transposed, count_ref, src_ref, dst_ref, edges_ref, first_ref, second_ref, out_ref, edge_buf, table, acc, sems
):
    slots = edge_buf.shape[0]
    count = count_ref[0]
    half = first_ref.shape[0]
    blocks = acc.shape[0] - 1
    for c in range(slots // CHUNK):

        @pl.when(c * CHUNK < count)
        def _():
            part = pl.ds(c * CHUNK, CHUNK)
            pltpu.make_async_copy(edges_ref.at[part], edge_buf.at[part], sems.at[c]).start()

    if second_ref is not None:
        table[:half] = first_ref[...]
        table[half:] = second_ref[...]
        source = table
    else:
        source = first_ref
    acc[...] = jnp.zeros_like(acc)
    contract = (((0,), (0,)), ((), ())) if transposed else (((1,), (0,)), ((), ()))

    for c in range(slots // CHUNK):

        @pl.when(c * CHUNK < count)
        def _():
            part = pl.ds(c * CHUNK, CHUNK)
            pltpu.make_async_copy(edges_ref.at[part], edge_buf.at[part], sems.at[c]).wait()

            def step(g, carry):
                base = c * CHUNK + g * GROUP
                products = []
                for u in range(GROUP + AHEAD):
                    if u < GROUP:
                        k = base + u
                        products.append(
                            lax.dot_general(
                                edge_buf[k], source[src_ref[k]], contract, preferred_element_type=jnp.float32
                            )
                        )
                    if u >= AHEAD:
                        k = base + u - AHEAD
                        place = jnp.where(k < count, dst_ref[k], blocks)
                        acc[place] += products[u - AHEAD]
                return carry

            lax.fori_loop(0, CHUNK // GROUP, step, 0)

    if len(out_ref.shape) == 3:
        out_ref[...] = acc[:blocks].astype(jnp.bfloat16)
    else:
        for z in range(blocks // 2):
            for h in range(2):
                out_ref[pl.ds(SPREAD * z + BSZ * h, BSZ)] = acc[2 * z + h].astype(jnp.bfloat16)
            if z < blocks // 2 - 1:
                out_ref[pl.ds(SPREAD * z + 2 * BSZ, 16)] = jnp.zeros((16, HID), jnp.bfloat16)


def spmm(transposed, count, src, dst, edges, first, second, blocks, out_shape):
    slots = edges.shape[0]
    vmem = pl.BlockSpec(memory_space=pltpu.VMEM)
    smem = pl.BlockSpec(memory_space=pltpu.SMEM)
    tables = [first] if second is None else [first, second]

    def body(count_ref, src_ref, dst_ref, edges_ref, *rest):
        first_ref = rest[0]
        second_ref = None if second is None else rest[1]
        out_ref, edge_buf, table, acc, sems = rest[len(tables) :]
        spmm_kernel(
            transposed, count_ref, src_ref, dst_ref, edges_ref, first_ref, second_ref, out_ref, edge_buf, table, acc, sems
        )

    table_rows = 1 if second is None else 2 * first.shape[0]
    return pl.pallas_call(
        body,
        out_shape=jax.ShapeDtypeStruct(out_shape, jnp.bfloat16),
        in_specs=[smem, smem, smem, pl.BlockSpec(memory_space=pl.ANY)] + [vmem] * len(tables),
        out_specs=vmem,
        scratch_shapes=[
            pltpu.VMEM((slots, BSZ, BSZ), jnp.bfloat16),
            pltpu.VMEM((table_rows, BSZ, HID), jnp.bfloat16),
            pltpu.VMEM((blocks + 1, BSZ, HID), jnp.float32),
            pltpu.SemaphoreType.DMA((slots // CHUNK,)),
        ],
        compiler_params=pltpu.CompilerParams(vmem_limit_bytes=48 * 1024 * 1024),
        cost_estimate=pl.CostEstimate(
            flops=2 * slots * BSZ * BSZ * HID, bytes_accessed=2 * slots * BSZ * BSZ, transcendentals=0
        ),
    )(count, src, dst, edges, *tables)


def per_row(row):
    square = jnp.broadcast_to(row, (BSZ, BSZ)).T
    return jnp.concatenate([square] * (HID // BSZ), axis=1)


def norm_of(counts_ref):
    return counts_ref[...].astype(jnp.float32) / QDEN


def end_kernel(parts_ref, counts_ref, out_ref):
    total = jnp.sum(parts_ref[...].astype(jnp.float32), axis=0)
    out_ref[...] = (total * per_row(norm_of(counts_ref))).astype(jnp.bfloat16)


def small_call(kernel, out_shape, *operands):
    vmem = pl.BlockSpec(memory_space=pltpu.VMEM)
    return pl.pallas_call(
        kernel,
        out_shape=out_shape,
        in_specs=[vmem] * len(operands),
        out_specs=jax.tree.map(lambda _: vmem, out_shape),
        compiler_params=pltpu.CompilerParams(vmem_limit_bytes=12 * 1024 * 1024),
    )(*operands)


def middle_kernel(
    sums_ref, received_ref, counts_ref, weight_ref, cotangent_ref, activated_ref, back_ref
):
    weight = weight_ref[...]
    largest = jnp.full((1, 1), 1e-30, jnp.float32)
    backs = []
    for h in range(2):
        mine = sums_ref[pl.ds(BSZ * h, BSZ)].astype(jnp.float32)
        total = mine + received_ref[pl.ds(BSZ * (1 - h), BSZ)].astype(jnp.float32)
        if h == 0:
            norm = per_row(norm_of(counts_ref))
            cotangent = cotangent_ref[...].astype(jnp.float32)
        else:
            norm = per_row(received_ref[pl.ds(3 * BSZ, 16)].astype(jnp.float32)[:1, :BSZ] / QDEN)
            cotangent = received_ref[pl.ds(2 * BSZ, BSZ)].astype(jnp.float32)
        aggregated = (total * norm).astype(jnp.bfloat16)
        preact = jnp.dot(aggregated, weight, preferred_element_type=jnp.float32)
        gate = jax.nn.sigmoid(preact)
        if h == 0:
            activated_ref[...] = (preact * gate).astype(jnp.bfloat16)
        slope = gate * (1.0 + preact * (1.0 - gate))
        dpre = (cotangent * slope).astype(jnp.bfloat16)
        back = lax.dot_general(dpre, weight, (((1,), (1,)), ((), ())), preferred_element_type=jnp.float32)
        back = (back * norm).astype(jnp.bfloat16).astype(jnp.float32)
        largest = jnp.maximum(largest, jnp.max(jnp.abs(back), axis=(0, 1), keepdims=True))
        backs.append(back)
    power = 14.0 - jnp.floor(jnp.log2(largest))
    for h in range(2):
        back_ref[pl.ds(BSZ * h, BSZ)] = backs[h] * jnp.exp2(power)
    back_ref[pl.ds(2 * BSZ, 8)] = jnp.broadcast_to(power, (8, HID))


def exchange(value, axes):
    return lax.all_to_all(value, axes, 0, 0, tiled=True)


def other_core(value):
    return lax.ppermute(value, "core", [(0, 1), (1, 0)])


def gather_scaled(value):
    sent = value.astype(jnp.float16)
    pairs = lax.all_gather(sent, ("zh", "zl"), axis=0, tiled=True).reshape(16, 2 * BSZ + 8, HID)
    back = jnp.exp2(-pairs[:, 2 * BSZ : 2 * BSZ + 1, :1].astype(jnp.float32))
    table = (pairs[:, : 2 * BSZ].astype(jnp.float32) * back).astype(jnp.bfloat16)
    return table.reshape(32, BSZ, HID)


def other_x(value):
    return lax.ppermute(value, "xl", [(0, 1), (1, 0)])


def summed_over_z(partial):
    shard = lax.psum_scatter(partial, ("zh", "zl"), scatter_dimension=0, tiled=True)
    shard = lax.optimization_barrier(shard)
    return lax.dynamic_slice(shard, (lax.axis_index(("zh", "zl")), 0), (2 * BSZ, HID))


def per_device(
    hidden_values, node_scale, node_weight, weight, cotangent, block_rows, block_cols, block_count, edge_counts
):
    core = lax.axis_index("core")
    counts = node_weight[None, :]
    edges = edge_counts[0, 0]
    rows = block_rows[0, 0]
    cols = block_cols[0, 0]
    count = block_count[0]
    row_at = (rows & ~1) + ((rows & 1) ^ lax.axis_index("xl"))
    col_at = ((cols & 1) ^ core) * 8 + (cols >> 1)

    factor = node_scale * (node_weight.astype(jnp.float32) / QDEN)
    scaled = (hidden_values.astype(jnp.float32) * factor[:, None]).astype(jnp.bfloat16)
    mine = exchange(jnp.broadcast_to(scaled[None], (8, BSZ, HID)), ("y", "xh"))
    theirs = other_core(mine)
    partial = spmm(True, count, col_at, row_at, edges, mine, theirs, 32, (16 * (SPREAD - 1), HID))
    sums = summed_over_z(partial)
    small = jnp.broadcast_to(jnp.tile(node_weight.astype(jnp.bfloat16), HID // BSZ), (16, HID))
    received = other_x(jnp.concatenate([sums, cotangent, small], axis=0))
    own = jax.ShapeDtypeStruct((BSZ, HID), jnp.bfloat16)
    sent = jax.ShapeDtypeStruct((2 * BSZ + 8, HID), jnp.float32)
    activated, back = small_call(middle_kernel, (own, sent), sums, received, counts, weight, cotangent)

    table = gather_scaled(back)
    partial = spmm(False, count, row_at, col_at, edges, table, None, 16, (16, BSZ, HID))
    received = other_core(partial[8:])
    pair = (partial[:8].astype(jnp.float32) + received.astype(jnp.float32)).astype(jnp.bfloat16)
    pair = exchange(pair, ("y", "xh"))
    grad_hidden = small_call(end_kernel, own, pair, counts)
    return activated, grad_hidden


def solution(mesh):
    fine = Mesh(mesh.devices.reshape(4, 2, 2, 8, 2, 2), NAMES)
    return jax.shard_map(
        per_device,
        mesh=fine,
        in_specs=(
            P(BLK + DOM, None),
            P(BLK + DOM),
            P(BLK + DOM),
            P(),
            P(BLK + DOM, None),
            P(BLK, DOM, None),
            P(BLK, DOM, None),
            P(BLK, DOM),
            P(BLK, DOM, None, None, None),
        ),
        out_specs=(P(BLK + DOM, None), P(BLK + DOM, None)),
        check_vma=False,
    )
```
